32 devices in a mesh: group: 2 (over y), row: 4 (over z), col: 2 (over x), tm: 2 (over core).
Axes of the slice: x: 2, y: 2, z: 4, core: 2. Of those that a mesh axis runs over, the one named last changes fastest.
Arguments:
- spectra: float32 [24, 32, 1024], P('tm', ('group', 'row', 'col')), parts along dimension 1, may hold values from -6 to 6
- station_block: int32 [32], P('group'), parts along dimension 0, may hold values from 0 to 15
- pair_mask: int32 [32, 16], P('group'), parts along dimension 0, may hold values 0 or 1
Outputs:
- linear_stack: float32 [32, 4, 2, 2, 1024], P(('group', 'row'), 'tm', 'col'), parts along dimension 0
- phase_stack: float32 [32, 4, 2, 2, 1024], P(('group', 'row'), 'tm', 'col'), parts along dimension 0
The draws below stay inside these ranges and needn't reach their ends.
There are 2 independent parts, one for each index of `group`. The reference program is written for one: setup_inputs(seed, part) draws one part's arguments, and reference() takes and returns one part's arrays. A program takes and returns all parts, laid end to end along the dimension named above; each array names one. Nothing has to cross between parts.
All inputs are finite; a program needn't handle non-finite values.
Results may differ from the reference program's by a relative error of at most 0.0029.
Values sent between devices are 32-bit elements; how exact they have to be, the bound alone decides.
A program may use at most 64 MiB of HBM per device.

```python
import math
import jax
import jax.numpy as jnp
from jax import lax

FREQS = 512
LAGS = 1024
STA_DEV = 2
BLOCKS = 16
WINDOWS = 24
STATIONS = 16
N_ROW = 4
N_COL = 2


def draw_spectra(key, part):
    key = jax.random.fold_in(key, 7)
    first_key, second_key = jax.random.split(key, 2)
    common = jax.random.normal(first_key, (STATIONS, 2 * FREQS), jnp.float32)
    noise = jax.random.normal(second_key, (WINDOWS, STATIONS, 2 * FREQS), jnp.float32)
    return jnp.clip(common[None] + 0.7 * noise, -6.0, 6.0).astype(jnp.float32)


def with_ends(entries, stream_key, least, high):
    spot = [jax.random.randint(jax.random.fold_in(stream_key, axis), (), 0, length) for axis, length in enumerate(entries.shape)]
    main_axis = entries.shape.index(max(entries.shape))
    beside = spot[:main_axis] + [(spot[main_axis] + 1) % entries.shape[main_axis]] + spot[main_axis + 1:]
    return entries.at[tuple(spot)].set(least).at[tuple(beside)].set(high)


def setup_inputs(seed: int = 0, part: int = 0) -> dict:
    arg_keys = jax.random.split(jax.random.key(seed), 4)
    part_keys = jax.random.split(jax.random.fold_in(arg_keys[3], part), 4)
    spectra = draw_spectra(jax.random.fold_in(jax.random.fold_in(arg_keys[3], part), 71), part)
    station_block = with_ends(jax.random.randint(part_keys[1], (STATIONS,), 0, BLOCKS), jax.random.fold_in(part_keys[1], 1), 0, BLOCKS - 1).astype(jnp.int32)
    pair_mask = with_ends((jax.random.randint(part_keys[2], (BLOCKS, BLOCKS), 0, 3) < 2).astype(jnp.int32), jax.random.fold_in(part_keys[2], 1), 0, 1)
    return dict(spectra=spectra, station_block=station_block, pair_mask=pair_mask)


def build_transform(bin_count):
    lag_count = 2 * bin_count
    phase_index = jnp.arange(bin_count, dtype=jnp.int32)[:, None] * jnp.arange(lag_count, dtype=jnp.int32)[None, :] % lag_count
    angles = phase_index.astype(jnp.float32) * (2.0 * math.pi / lag_count)
    cosine_values = jnp.cos(angles)
    sine_values = jnp.sin(angles)
    upper_half = jnp.concatenate([cosine_values, sine_values], 1)
    lower_half = jnp.concatenate([-sine_values, cosine_values], 1)
    return (jnp.concatenate([upper_half, lower_half], 0) * (1.0 / (3.0 * math.sqrt(bin_count)))).astype(jnp.bfloat16)

def window_terms(left_side, right_side, transform):
    bin_count = left_side.shape[1] // 2
    left_real, left_imag = (left_side[:, :bin_count], left_side[:, bin_count:])
    right_real, right_imag = (right_side[:, :bin_count], right_side[:, bin_count:])
    real_cross = left_real[:, None, :] * right_real[None] + left_imag[:, None, :] * right_imag[None]
    imag_cross = left_imag[:, None, :] * right_real[None] - left_real[:, None, :] * right_imag[None]
    cross_spectra = jnp.concatenate([real_cross, imag_cross], -1).astype(jnp.bfloat16)
    cross_spectra = cross_spectra.reshape(left_side.shape[0] * right_side.shape[0], 2 * bin_count)
    analytic = jnp.dot(cross_spectra, transform, preferred_element_type=jnp.float32)
    lag_count = transform.shape[1] // 2
    real_part, imag_part = (analytic[:, :lag_count], analytic[:, lag_count:])
    magnitude = jnp.maximum(jnp.sqrt(real_part * real_part + imag_part * imag_part), 0.5)
    return (real_part, real_part / magnitude, imag_part / magnitude)

def stack_windows(left_side, right_side, transform):
    rows_first = left_side.shape[1]
    rows_second = right_side.shape[1]
    lag_count = transform.shape[1] // 2
    initial = (jnp.zeros((rows_first * rows_second, lag_count), jnp.float32), jnp.zeros((rows_first * rows_second, lag_count), jnp.float32), jnp.zeros((rows_first * rows_second, lag_count), jnp.float32))

    def accumulate(totals, window):
        terms = window_terms(window[0], window[1], transform)
        return ((totals[0] + terms[0], totals[1] + terms[1], totals[2] + terms[2]), None)
    totals, ignored = lax.scan(accumulate, initial, (left_side, right_side))
    return tuple((part.reshape(rows_first, rows_second, lag_count) for part in totals))

def reference(spectra, station_block, pair_mask):
    transform = build_transform(FREQS)
    stack_sum, phase_real, phase_imag = stack_windows(spectra, spectra, transform)
    labels = jnp.arange(BLOCKS, dtype=jnp.int32)
    onehot_rows = (station_block[:, None] == labels[None, :]).astype(jnp.float32)
    kept_pairs = jnp.dot(jnp.dot(onehot_rows, pair_mask.astype(jnp.float32), preferred_element_type=jnp.float32), onehot_rows.T, preferred_element_type=jnp.float32)
    linear = kept_pairs[:, :, None] * stack_sum / WINDOWS
    weighted = linear * (phase_real * phase_real + phase_imag * phase_imag) / (WINDOWS * WINDOWS)
    out_shape = (STATIONS, N_ROW, N_COL, STA_DEV, LAGS)
    return (linear.reshape(out_shape), weighted.reshape(out_shape))
```

```python
import functools
import math

import jax
import jax.numpy as jnp
import ml_dtypes
import numpy as np
from jax import lax
from jax.experimental import pallas as pl
from jax.experimental.pallas import tpu as pltpu
from jax.sharding import PartitionSpec as P

MESH = pl.DeviceIdType.MESH


def transform_table(bin_count):
    lag_count = 2 * bin_count
    phase_index = np.arange(bin_count)[:, None] * np.arange(lag_count)[None, :] % lag_count
    angles = phase_index * (2.0 * math.pi / lag_count)
    cosine, sine = np.cos(angles), np.sin(angles)
    table = np.concatenate(
        [np.concatenate([cosine, sine], 1), np.concatenate([-sine, cosine], 1)], 0
    )
    table = table / (3.0 * math.sqrt(bin_count))
    return table.astype(np.float32).astype(ml_dtypes.bfloat16)


def kernel(
    n_row, n_col, owned, labels_ref, mask_ref, spectra_ref, table_hbm, linear_ref, phase_ref,
    blocks, table, cross, table_sem, send_sem, recv_sem,
):
    half = n_row // 2
    row, col, core = lax.axis_index("row"), lax.axis_index("col"), lax.axis_index("tm")
    windows_here = spectra_ref.shape[0]
    rows = windows_here * owned
    bins = spectra_ref.shape[2] // 2
    lags = 2 * bins
    windows = 2 * windows_here
    base = core * half
    other = 1 - core
    home = row // half
    lane = row % half

    table_copy = pltpu.make_async_copy(table_hbm, table, table_sem)
    table_copy.start()

    barrier = pltpu.get_barrier_semaphore()
    pl.semaphore_signal(barrier, inc=1, device_id={"tm": other}, device_id_type=MESH)
    for step in range(1, n_col):
        for t in range(2):
            pl.semaphore_signal(
                barrier, inc=1, device_id={"col": (col + step) % n_col, "tm": t},
                device_id_type=MESH,
            )
    for a in range(half):
        @pl.when(base + a != row)
        def _():
            for t in range(2):
                pl.semaphore_signal(
                    barrier, inc=1, device_id={"row": base + a, "tm": t}, device_id_type=MESH
                )

    blocks[col, core] = spectra_ref[...].reshape(rows, 2 * bins)
    pl.semaphore_wait(barrier, 1 + 2 * (n_col - 1) + (n_row - 1))

    mine = blocks.at[col, core]
    copies = []

    def send(slot, where):
        copy = pltpu.make_async_remote_copy(
            src_ref=mine, dst_ref=blocks.at[slot, core], send_sem=send_sem.at[len(copies)],
            recv_sem=recv_sem.at[slot, core], device_id=where, device_id_type=MESH,
        )
        copy.start()
        copies.append(copy)

    for step in sorted(range(1, n_row), key=lambda s: abs(s - half)):
        send(n_col + lane, {"row": (row + step) % n_row, "tm": home})
    for step in range(1, n_col):
        for t in range(2):
            send(col, {"col": (col + step) % n_col, "tm": t})
    send(col, {"tm": other})

    def arrived(slot, h):
        pltpu.make_async_copy(mine, blocks.at[slot, h], recv_sem.at[slot, h]).wait()

    arrived(col, other)
    for step in range(1, n_col):
        for h in range(2):
            arrived((col + step) % n_col, h)

    odd = lax.broadcasted_iota(jnp.int32, (rows, 2 * bins), 0) % 2 == 1
    start = jnp.clip(row - base, 0, half - 1)
    group_rows = lax.broadcasted_iota(jnp.int32, (8, 1), 0)

    def one_row(index, carry):
        a = (start + index) % half
        away = base + a != row
        slot = jnp.where(away, n_col + a, col)

        @pl.when(away)
        def _():
            for h in range(2):
                arrived(n_col + a, h)

        for h in range(2):
            right = blocks[slot, h]
            right_real, right_imag = right[:, :bins], right[:, bins:]
            for c in range(n_col):
                left = blocks[c, h]
                for s in range(2):
                    if s:
                        left = jnp.where(
                            odd, pltpu.roll(left, 1, 0), pltpu.roll(left, rows - 1, 0)
                        )
                    left_real, left_imag = left[:, :bins], left[:, bins:]
                    at = pl.ds(((h * n_col + c) * 2 + s) * rows, rows)
                    cross[at, :bins] = (
                        left_real * right_real + left_imag * right_imag
                    ).astype(jnp.bfloat16)
                    cross[at, bins:] = (
                        left_imag * right_real - left_real * right_imag
                    ).astype(jnp.bfloat16)

        @pl.when(index == 0)
        def _():
            table_copy.wait()

        scales = []
        for pair in range(n_col // 2):
            scale = jnp.zeros((8, 1), jnp.float32)
            for p in range(8):
                first = labels_ref[row * n_col * owned + pair * 4 + p // 2]
                second = labels_ref[((base + a) * n_col + col) * owned + p % 2]
                kept = mask_ref[first, second].astype(jnp.float32)
                scale = jnp.where(group_rows == p, kept, scale)
            scales.append(scale)

        tile = 256

        def one_tile(j, carry):
            at = pl.ds(pl.multiple_of(j * tile, tile), tile)
            at_imag = pl.ds(pl.multiple_of(lags + j * tile, tile), tile)
            real = jnp.dot(cross[...], table[:, at], preferred_element_type=jnp.float32)
            imag = jnp.dot(cross[...], table[:, at_imag], preferred_element_type=jnp.float32)
            inverse = jnp.minimum(lax.rsqrt(real * real + imag * imag), 2.0)

            def total(part):
                part = part.reshape(2, n_col, 2, rows // 8, 8, tile).sum(axis=(0, 3))
                out = []
                for pair in range(n_col // 2):
                    whole = []
                    for s in range(2):
                        upper, lower = part[2 * pair, s], part[2 * pair + 1, s]
                        upper = upper + pltpu.roll(upper, 4, 0)
                        lower = lower + pltpu.roll(lower, 4, 0)
                        both = jnp.where(group_rows < 4, upper, lower)
                        whole.append(
                            both
                            + jnp.where(
                                group_rows % 4 < 2, pltpu.roll(both, 6, 0), pltpu.roll(both, 2, 0)
                            )
                        )
                    straight = (group_rows % 4 == 0) | (group_rows % 4 == 3)
                    out.append(jnp.where(straight, whole[0], whole[1]))
                return out

            stack, phase_real, phase_imag = total(real), total(real * inverse), total(imag * inverse)
            for pair in range(n_col // 2):
                linear = stack[pair] * scales[pair] * (1.0 / windows)
                power = phase_real[pair] * phase_real[pair] + phase_imag[pair] * phase_imag[pair]
                linear_ref[a, pl.ds(8 * pair, 8), at] = linear
                phase_ref[a, pl.ds(8 * pair, 8), at] = linear * power * (1.0 / (windows * windows))
            return carry

        lax.fori_loop(0, lags // tile, one_tile, 0)
        return carry

    lax.fori_loop(0, half, one_row, 0)

    for copy in copies:
        copy.wait_send()


def on_device(n_row, n_col, table, spectra, station_block, pair_mask):
    windows_here, owned, width = spectra.shape
    half = n_row // 2
    rows = windows_here * owned
    lags = width
    first = n_col * owned
    shape = jax.ShapeDtypeStruct((half, first * owned, lags), jnp.float32)
    sends = 1 + 2 * (n_col - 1) + (n_row - 1)
    linear, phase = pl.pallas_call(
        functools.partial(kernel, n_row, n_col, owned),
        out_shape=(shape, shape),
        in_specs=[
            pl.BlockSpec(memory_space=pltpu.SMEM),
            pl.BlockSpec(memory_space=pltpu.SMEM),
            pl.BlockSpec(memory_space=pltpu.VMEM),
            pl.BlockSpec(memory_space=pl.ANY),
        ],
        out_specs=[pl.BlockSpec(memory_space=pltpu.VMEM)] * 2,
        scratch_shapes=[
            pltpu.VMEM((n_col + half, 2, rows, width), jnp.float32),
            pltpu.VMEM(table.shape, jnp.bfloat16),
            pltpu.VMEM((4 * n_col * rows, width), jnp.bfloat16),
            pltpu.SemaphoreType.DMA,
            pltpu.SemaphoreType.DMA((sends,)),
            pltpu.SemaphoreType.DMA((n_col + half, 2)),
        ],
        compiler_params=pltpu.CompilerParams(
            collective_id=0, has_side_effects=True, vmem_limit_bytes=48 * 1024 * 1024
        ),
    )(station_block, pair_mask, spectra, jnp.asarray(table))

    def placed(part):
        part = part.reshape(half, first, owned, lags)
        return part.transpose(1, 0, 2, 3)[:, :, None]

    return placed(linear), placed(phase)


def solution(mesh):
    def program(spectra, station_block, pair_mask):
        table = transform_table(spectra.shape[2] // 2)
        in_specs = (P("tm", ("group", "row", "col"), None), P("group"), P("group", None))
        out_specs = (
            P(("group", "row"), "tm", "col", None, None),
            P(("group", "row"), "tm", "col", None, None),
        )
        return jax.shard_map(
            functools.partial(on_device, mesh.shape["row"], mesh.shape["col"], table),
            mesh=mesh, in_specs=in_specs, out_specs=out_specs, check_vma=False,
        )(spectra, station_block, pair_mask)

    return program
```

```python
import functools
import math

import jax
import jax.numpy as jnp
import ml_dtypes
import numpy as np
from jax import lax
from jax.experimental import pallas as pl
from jax.experimental.pallas import tpu as pltpu
from jax.sharding import PartitionSpec as P

MESH = pl.DeviceIdType.MESH


def transform_table(bin_count):
    lag_count = 2 * bin_count
    phase_index = np.arange(bin_count)[:, None] * np.arange(lag_count)[None, :] % lag_count
    angles = phase_index * (2.0 * math.pi / lag_count)
    cosine, sine = np.cos(angles), np.sin(angles)
    table = np.concatenate(
        [np.concatenate([cosine, sine], 1), np.concatenate([-sine, cosine], 1)], 0
    )
    table = table / (3.0 * math.sqrt(bin_count))
    return table.astype(np.float32).astype(ml_dtypes.bfloat16)


def kernel(
    n_row, n_col, owned, labels_hbm, mask_hbm, spectra_hbm, table_hbm, linear_ref, phase_ref,
    blocks, table, cross, spectra_ref, labels_ref, mask_ref, local_sem, send_sem, recv_sem,
):
    half = n_row // 2
    row, col, core = lax.axis_index("row"), lax.axis_index("col"), lax.axis_index("tm")
    windows_here = spectra_ref.shape[0]
    rows = windows_here * owned
    bins = spectra_ref.shape[2] // 2
    lags = 2 * bins
    windows = 2 * windows_here
    base = core * half
    other = 1 - core
    home = row // half
    lane = row % half

    spectra_copy = pltpu.make_async_copy(spectra_hbm, spectra_ref, local_sem.at[0])
    spectra_copy.start()
    labels_copy = pltpu.make_async_copy(labels_hbm, labels_ref, local_sem.at[1])
    labels_copy.start()
    mask_copy = pltpu.make_async_copy(mask_hbm, mask_ref, local_sem.at[2])
    mask_copy.start()
    table_copy = pltpu.make_async_copy(table_hbm, table, local_sem.at[3])
    table_copy.start()

    barrier = pltpu.get_barrier_semaphore()
    pl.semaphore_signal(barrier, inc=1, device_id={"tm": other}, device_id_type=MESH)
    for step in range(1, n_col):
        for t in range(2):
            pl.semaphore_signal(
                barrier, inc=1, device_id={"col": (col + step) % n_col, "tm": t},
                device_id_type=MESH,
            )
    for a in range(half):
        @pl.when(base + a != row)
        def _():
            for t in range(2):
                pl.semaphore_signal(
                    barrier, inc=1, device_id={"row": base + a, "tm": t}, device_id_type=MESH
                )

    spectra_copy.wait()
    blocks[col, core] = spectra_ref[...].reshape(rows, 2 * bins)
    pl.semaphore_wait(barrier, 1 + 2 * (n_col - 1) + (n_row - 1))

    mine = blocks.at[col, core]
    copies = []

    def send(slot, where):
        copy = pltpu.make_async_remote_copy(
            src_ref=mine, dst_ref=blocks.at[slot, core], send_sem=send_sem.at[len(copies)],
            recv_sem=recv_sem.at[slot, core], device_id=where, device_id_type=MESH,
        )
        copy.start()
        copies.append(copy)

    for step in sorted(range(1, n_row), key=lambda s: abs(s - half)):
        send(n_col + lane, {"row": (row + step) % n_row, "tm": home})
    for step in range(1, n_col):
        for t in range(2):
            send(col, {"col": (col + step) % n_col, "tm": t})
    send(col, {"tm": other})

    def arrived(slot, h):
        pltpu.make_async_copy(mine, blocks.at[slot, h], recv_sem.at[slot, h]).wait()

    labels_copy.wait()
    mask_copy.wait()
    arrived(col, other)
    for step in range(1, n_col):
        for h in range(2):
            arrived((col + step) % n_col, h)

    odd = lax.broadcasted_iota(jnp.int32, (rows, 2 * bins), 0) % 2 == 1
    start = jnp.clip(row - base, 0, half - 1)
    group_rows = lax.broadcasted_iota(jnp.int32, (8, 1), 0)

    def one_row(index, carry):
        a = (start + index) % half
        away = base + a != row
        slot = jnp.where(away, n_col + a, col)

        @pl.when(away)
        def _():
            for h in range(2):
                arrived(n_col + a, h)

        for h in range(2):
            right = blocks[slot, h]
            right_real, right_imag = right[:, :bins], right[:, bins:]
            for c in range(n_col):
                left = blocks[c, h]
                for s in range(2):
                    if s:
                        left = jnp.where(
                            odd, pltpu.roll(left, 1, 0), pltpu.roll(left, rows - 1, 0)
                        )
                    left_real, left_imag = left[:, :bins], left[:, bins:]
                    at = pl.ds(((h * n_col + c) * 2 + s) * rows, rows)
                    cross[at, :bins] = (
                        left_real * right_real + left_imag * right_imag
                    ).astype(jnp.bfloat16)
                    cross[at, bins:] = (
                        left_imag * right_real - left_real * right_imag
                    ).astype(jnp.bfloat16)

        @pl.when(index == 0)
        def _():
            table_copy.wait()

        scales = []
        for pair in range(n_col // 2):
            scale = jnp.zeros((8, 1), jnp.float32)
            for p in range(8):
                first = labels_ref[row * n_col * owned + pair * 4 + p // 2]
                second = labels_ref[((base + a) * n_col + col) * owned + p % 2]
                kept = mask_ref[first, second].astype(jnp.float32)
                scale = jnp.where(group_rows == p, kept, scale)
            scales.append(scale)

        tile = 256

        def one_tile(j, carry):
            at = pl.ds(pl.multiple_of(j * tile, tile), tile)
            at_imag = pl.ds(pl.multiple_of(lags + j * tile, tile), tile)
            real = jnp.dot(cross[...], table[:, at], preferred_element_type=jnp.float32)
            imag = jnp.dot(cross[...], table[:, at_imag], preferred_element_type=jnp.float32)
            inverse = jnp.minimum(lax.rsqrt(real * real + imag * imag), 2.0)

            def total(part):
                part = part.reshape(2, n_col, 2, rows // 8, 8, tile).sum(axis=(0, 3))
                out = []
                for pair in range(n_col // 2):
                    whole = []
                    for s in range(2):
                        upper, lower = part[2 * pair, s], part[2 * pair + 1, s]
                        upper = upper + pltpu.roll(upper, 4, 0)
                        lower = lower + pltpu.roll(lower, 4, 0)
                        both = jnp.where(group_rows < 4, upper, lower)
                        whole.append(
                            both
                            + jnp.where(
                                group_rows % 4 < 2, pltpu.roll(both, 6, 0), pltpu.roll(both, 2, 0)
                            )
                        )
                    straight = (group_rows % 4 == 0) | (group_rows % 4 == 3)
                    out.append(jnp.where(straight, whole[0], whole[1]))
                return out

            stack, phase_real, phase_imag = total(real), total(real * inverse), total(imag * inverse)
            for pair in range(n_col // 2):
                linear = stack[pair] * scales[pair] * (1.0 / windows)
                power = phase_real[pair] * phase_real[pair] + phase_imag[pair] * phase_imag[pair]
                linear_ref[a, pl.ds(8 * pair, 8), at] = linear
                phase_ref[a, pl.ds(8 * pair, 8), at] = linear * power * (1.0 / (windows * windows))
            return carry

        lax.fori_loop(0, lags // tile, one_tile, 0, unroll=True)
        return carry

    lax.fori_loop(0, half, one_row, 0)

    for copy in copies:
        copy.wait_send()


def on_device(n_row, n_col, table, spectra, station_block, pair_mask):
    windows_here, owned, width = spectra.shape
    half = n_row // 2
    rows = windows_here * owned
    lags = width
    first = n_col * owned
    shape = pltpu.VMEM((half, first * owned, lags), jnp.float32)
    sends = 1 + 2 * (n_col - 1) + (n_row - 1)
    linear, phase = pl.pallas_call(
        functools.partial(kernel, n_row, n_col, owned),
        out_shape=(shape, shape),
        in_specs=[
            pl.BlockSpec(memory_space=pltpu.HBM),
        ] * 4,
        out_specs=[pl.BlockSpec(memory_space=pltpu.VMEM)] * 2,
        scratch_shapes=[
            pltpu.VMEM((n_col + half, 2, rows, width), jnp.float32),
            pltpu.VMEM(table.shape, jnp.bfloat16),
            pltpu.VMEM((4 * n_col * rows, width), jnp.bfloat16),
            pltpu.VMEM(spectra.shape, jnp.float32),
            pltpu.SMEM(station_block.shape, jnp.int32),
            pltpu.SMEM(pair_mask.shape, jnp.int32),
            pltpu.SemaphoreType.DMA((4,)),
            pltpu.SemaphoreType.DMA((sends,)),
            pltpu.SemaphoreType.DMA((n_col + half, 2)),
        ],
        compiler_params=pltpu.CompilerParams(
            collective_id=0, has_side_effects=True, vmem_limit_bytes=48 * 1024 * 1024
        ),
    )(
        *(
            pltpu.with_memory_space_constraint(part, pltpu.HBM)
            for part in (station_block, pair_mask, spectra, jnp.asarray(table))
        )
    )

    def placed(part):
        part = part.reshape(half, first, owned, lags)
        return part.transpose(1, 0, 2, 3)[:, :, None]

    return placed(linear), placed(phase)


def solution(mesh):
    def program(spectra, station_block, pair_mask):
        table = transform_table(spectra.shape[2] // 2)
        in_specs = (P("tm", ("group", "row", "col"), None), P("group"), P("group", None))
        out_specs = (
            P(("group", "row"), "tm", "col", None, None),
            P(("group", "row"), "tm", "col", None, None),
        )
        return jax.shard_map(
            functools.partial(on_device, mesh.shape["row"], mesh.shape["col"], table),
            mesh=mesh, in_specs=in_specs, out_specs=out_specs, check_vma=False,
        )(spectra, station_block, pair_mask)

    return program
```

```python
import functools
import math

import jax
import jax.numpy as jnp
import ml_dtypes
import numpy as np
from jax import lax
from jax.experimental import pallas as pl
from jax.experimental.pallas import tpu as pltpu
from jax.sharding import PartitionSpec as P

MESH = pl.DeviceIdType.MESH


def transform_table(bin_count):
    lag_count = 2 * bin_count
    phase_index = np.arange(bin_count)[:, None] * np.arange(lag_count)[None, :] % lag_count
    angles = phase_index * (2.0 * math.pi / lag_count)
    cosine, sine = np.cos(angles), np.sin(angles)
    table = np.concatenate(
        [np.concatenate([cosine, sine], 1), np.concatenate([-sine, cosine], 1)], 0
    )
    table = table / (3.0 * math.sqrt(bin_count))
    return table.astype(np.float32).astype(ml_dtypes.bfloat16)


def kernel(
    n_row, n_col, owned, labels_hbm, mask_hbm, spectra_hbm, table_hbm, linear_ref, phase_ref,
    blocks, swapped, table, cross, spectra_ref, labels_ref, mask_ref, local_sem, send_sem, recv_sem,
):
    half = n_row // 2
    row, col, core = lax.axis_index("row"), lax.axis_index("col"), lax.axis_index("tm")
    windows_here = spectra_ref.shape[0]
    rows = windows_here * owned
    bins = spectra_ref.shape[2] // 2
    lags = 2 * bins
    windows = 2 * windows_here
    base = core * half
    other = 1 - core
    home = row // half
    lane = row % half

    spectra_copy = pltpu.make_async_copy(spectra_hbm, spectra_ref, local_sem.at[0])
    spectra_copy.start()
    labels_copy = pltpu.make_async_copy(labels_hbm, labels_ref, local_sem.at[1])
    labels_copy.start()
    mask_copy = pltpu.make_async_copy(mask_hbm, mask_ref, local_sem.at[2])
    mask_copy.start()
    table_copy = pltpu.make_async_copy(table_hbm, table, local_sem.at[3])
    table_copy.start()

    barrier = pltpu.get_barrier_semaphore()
    pl.semaphore_signal(barrier, inc=1, device_id={"tm": other}, device_id_type=MESH)
    for step in range(1, n_col):
        for t in range(2):
            pl.semaphore_signal(
                barrier, inc=1, device_id={"col": (col + step) % n_col, "tm": t},
                device_id_type=MESH,
            )
    for a in range(half):
        @pl.when(base + a != row)
        def _():
            for t in range(2):
                pl.semaphore_signal(
                    barrier, inc=1, device_id={"row": base + a, "tm": t}, device_id_type=MESH
                )

    spectra_copy.wait()
    blocks[col, core] = spectra_ref[...].reshape(rows, 2 * bins)
    pl.semaphore_wait(barrier, 1 + 2 * (n_col - 1) + (n_row - 1))

    mine = blocks.at[col, core]
    copies = []

    def send(slot, where):
        copy = pltpu.make_async_remote_copy(
            src_ref=mine, dst_ref=blocks.at[slot, core], send_sem=send_sem.at[len(copies)],
            recv_sem=recv_sem.at[slot, core], device_id=where, device_id_type=MESH,
        )
        copy.start()
        copies.append(copy)

    for step in sorted(range(1, n_row), key=lambda s: abs(s - half)):
        send(n_col + lane, {"row": (row + step) % n_row, "tm": home})
    for step in range(1, n_col):
        for t in range(2):
            send(col, {"col": (col + step) % n_col, "tm": t})
    send(col, {"tm": other})

    def arrived(slot, h):
        pltpu.make_async_copy(mine, blocks.at[slot, h], recv_sem.at[slot, h]).wait()

    labels_copy.wait()
    mask_copy.wait()
    arrived(col, other)
    for step in range(1, n_col):
        for h in range(2):
            arrived((col + step) % n_col, h)

    odd = lax.broadcasted_iota(jnp.int32, (rows, 2 * bins), 0) % 2 == 1
    for h in range(2):
        for c in range(n_col):
            left = blocks[c, h]
            swapped[c, h] = jnp.where(odd, pltpu.roll(left, 1, 0), pltpu.roll(left, rows - 1, 0))
    table_copy.wait()
    start = jnp.clip(row - base, 0, half - 1)
    group_rows = lax.broadcasted_iota(jnp.int32, (8, 1), 0)

    def one_row(index, carry):
        a = (start + index) % half
        away = base + a != row
        slot = jnp.where(away, n_col + a, col)

        scales = []
        for pair in range(n_col // 2):
            scale = jnp.zeros((8, 1), jnp.float32)
            for p in range(8):
                first = labels_ref[row * n_col * owned + pair * 4 + p // 2]
                second = labels_ref[((base + a) * n_col + col) * owned + p % 2]
                kept = mask_ref[first, second].astype(jnp.float32)
                scale = jnp.where(group_rows == p, kept, scale)
            scales.append(scale)

        @pl.when(away)
        def _():
            for h in range(2):
                arrived(n_col + a, h)

        for h in range(2):
            right = blocks[slot, h]
            right_real, right_imag = right[:, :bins], right[:, bins:]
            for c in range(n_col):
                left = blocks[c, h]
                for s in range(2):
                    if s:
                        left = swapped[c, h]
                    left_real, left_imag = left[:, :bins], left[:, bins:]
                    at = pl.ds(((h * n_col + c) * 2 + s) * rows, rows)
                    cross[at, :bins] = (
                        left_real * right_real + left_imag * right_imag
                    ).astype(jnp.bfloat16)
                    cross[at, bins:] = (
                        left_imag * right_real - left_real * right_imag
                    ).astype(jnp.bfloat16)

        tile = 512

        def one_tile(j, carry):
            at = pl.ds(pl.multiple_of(j * tile, tile), tile)
            at_imag = pl.ds(pl.multiple_of(lags + j * tile, tile), tile)
            real = jnp.dot(cross[...], table[:, at], preferred_element_type=jnp.float32)
            imag = jnp.dot(cross[...], table[:, at_imag], preferred_element_type=jnp.float32)
            inverse = jnp.minimum(lax.rsqrt(real * real + imag * imag), 2.0)

            def total(part):
                part = part.reshape(2, n_col, 2, rows // 8, 8, tile).sum(axis=(0, 3))
                out = []
                for pair in range(n_col // 2):
                    whole = []
                    for s in range(2):
                        upper, lower = part[2 * pair, s], part[2 * pair + 1, s]
                        upper = upper + pltpu.roll(upper, 4, 0)
                        lower = lower + pltpu.roll(lower, 4, 0)
                        both = jnp.where(group_rows < 4, upper, lower)
                        whole.append(
                            both
                            + jnp.where(
                                group_rows % 4 < 2, pltpu.roll(both, 6, 0), pltpu.roll(both, 2, 0)
                            )
                        )
                    straight = (group_rows % 4 == 0) | (group_rows % 4 == 3)
                    out.append(jnp.where(straight, whole[0], whole[1]))
                return out

            stack, phase_real, phase_imag = total(real), total(real * inverse), total(imag * inverse)
            for pair in range(n_col // 2):
                linear = stack[pair] * scales[pair] * (1.0 / windows)
                power = phase_real[pair] * phase_real[pair] + phase_imag[pair] * phase_imag[pair]
                linear_ref[a, pl.ds(8 * pair, 8), at] = linear
                phase_ref[a, pl.ds(8 * pair, 8), at] = linear * power * (1.0 / (windows * windows))
            return carry

        lax.fori_loop(0, lags // tile, one_tile, 0, unroll=True)
        return carry

    lax.fori_loop(0, half, one_row, 0)

    for copy in copies:
        copy.wait_send()


def on_device(n_row, n_col, table, spectra, station_block, pair_mask):
    windows_here, owned, width = spectra.shape
    half = n_row // 2
    rows = windows_here * owned
    lags = width
    first = n_col * owned
    shape = pltpu.VMEM((half, first * owned, lags), jnp.float32)
    sends = 1 + 2 * (n_col - 1) + (n_row - 1)
    linear, phase = pl.pallas_call(
        functools.partial(kernel, n_row, n_col, owned),
        out_shape=(shape, shape),
        in_specs=[
            pl.BlockSpec(memory_space=pltpu.HBM),
        ] * 4,
        out_specs=[pl.BlockSpec(memory_space=pltpu.VMEM)] * 2,
        scratch_shapes=[
            pltpu.VMEM((n_col + half, 2, rows, width), jnp.float32),
            pltpu.VMEM((n_col, 2, rows, width), jnp.float32),
            pltpu.VMEM(table.shape, jnp.bfloat16),
            pltpu.VMEM((4 * n_col * rows, width), jnp.bfloat16),
            pltpu.VMEM(spectra.shape, jnp.float32),
            pltpu.SMEM(station_block.shape, jnp.int32),
            pltpu.SMEM(pair_mask.shape, jnp.int32),
            pltpu.SemaphoreType.DMA((4,)),
            pltpu.SemaphoreType.DMA((sends,)),
            pltpu.SemaphoreType.DMA((n_col + half, 2)),
        ],
        compiler_params=pltpu.CompilerParams(
            collective_id=0, has_side_effects=True, vmem_limit_bytes=48 * 1024 * 1024
        ),
    )(
        *(
            pltpu.with_memory_space_constraint(part, pltpu.HBM)
            for part in (station_block, pair_mask, spectra, jnp.asarray(table))
        )
    )

    def placed(part):
        part = part.reshape(half, first, owned, lags)
        return part.transpose(1, 0, 2, 3)[:, :, None]

    return placed(linear), placed(phase)


def solution(mesh):
    def program(spectra, station_block, pair_mask):
        table = transform_table(spectra.shape[2] // 2)
        in_specs = (P("tm", ("group", "row", "col"), None), P("group"), P("group", None))
        out_specs = (
            P(("group", "row"), "tm", "col", None, None),
            P(("group", "row"), "tm", "col", None, None),
        )
        return jax.shard_map(
            functools.partial(on_device, mesh.shape["row"], mesh.shape["col"], table),
            mesh=mesh, in_specs=in_specs, out_specs=out_specs, check_vma=False,
        )(spectra, station_block, pair_mask)

    return program
```

```python
import functools
import math

import jax
import jax.numpy as jnp
import ml_dtypes
import numpy as np
from jax import lax
from jax.experimental import pallas as pl
from jax.experimental.pallas import tpu as pltpu
from jax.sharding import PartitionSpec as P

MESH = pl.DeviceIdType.MESH


def transform_table(bin_count):
    lag_count = 2 * bin_count
    phase_index = np.arange(bin_count)[:, None] * np.arange(lag_count)[None, :] % lag_count
    angles = phase_index * (2.0 * math.pi / lag_count)
    cosine, sine = np.cos(angles), np.sin(angles)
    table = np.concatenate(
        [np.concatenate([cosine, sine], 1), np.concatenate([-sine, cosine], 1)], 0
    )
    table = table / (3.0 * math.sqrt(bin_count))
    return table.astype(np.float32).astype(ml_dtypes.bfloat16)


def kernel(
    n_row, n_col, owned, labels_hbm, mask_hbm, spectra_hbm, table_hbm, linear_ref, phase_ref,
    blocks, swapped, table, cross, spectra_ref, labels_ref, mask_ref, local_sem, send_sem, recv_sem,
):
    half = n_row // 2
    row, col, core = lax.axis_index("row"), lax.axis_index("col"), lax.axis_index("tm")
    windows_here = spectra_ref.shape[0]
    rows = windows_here * owned
    bins = spectra_ref.shape[2] // 2
    lags = 2 * bins
    windows = 2 * windows_here
    base = core * half
    other = 1 - core
    home = row // half
    lane = row % half

    spectra_copy = pltpu.make_async_copy(spectra_hbm, spectra_ref, local_sem.at[0])
    spectra_copy.start()
    labels_copy = pltpu.make_async_copy(labels_hbm, labels_ref, local_sem.at[1])
    labels_copy.start()
    mask_copy = pltpu.make_async_copy(mask_hbm, mask_ref, local_sem.at[2])
    mask_copy.start()
    table_copy = pltpu.make_async_copy(table_hbm, table, local_sem.at[3])
    table_copy.start()

    barrier = pltpu.get_barrier_semaphore()
    pl.semaphore_signal(barrier, inc=1, device_id={"tm": other}, device_id_type=MESH)
    for step in range(1, n_col):
        for t in range(2):
            pl.semaphore_signal(
                barrier, inc=1, device_id={"col": (col + step) % n_col, "tm": t},
                device_id_type=MESH,
            )
    for a in range(half):
        @pl.when(base + a != row)
        def _():
            for t in range(2):
                pl.semaphore_signal(
                    barrier, inc=1, device_id={"row": base + a, "tm": t}, device_id_type=MESH
                )

    spectra_copy.wait()
    blocks[col, core] = spectra_ref[...].reshape(rows, 2 * bins)
    pl.semaphore_wait(barrier, 1 + 2 * (n_col - 1) + (n_row - 1))

    mine = blocks.at[col, core]
    copies = []

    def send(slot, where):
        copy = pltpu.make_async_remote_copy(
            src_ref=mine, dst_ref=blocks.at[slot, core], send_sem=send_sem.at[len(copies)],
            recv_sem=recv_sem.at[slot, core], device_id=where, device_id_type=MESH,
        )
        copy.start()
        copies.append(copy)

    for step in sorted(range(1, n_row), key=lambda s: abs(s - half)):
        send(n_col + lane, {"row": (row + step) % n_row, "tm": home})
    for step in range(1, n_col):
        for t in range(2):
            send(col, {"col": (col + step) % n_col, "tm": t})
    send(col, {"tm": other})

    def arrived(slot, h):
        pltpu.make_async_copy(mine, blocks.at[slot, h], recv_sem.at[slot, h]).wait()

    labels_copy.wait()
    mask_copy.wait()
    arrived(col, other)
    for step in range(1, n_col):
        for h in range(2):
            arrived((col + step) % n_col, h)

    odd = lax.broadcasted_iota(jnp.int32, (rows, 2 * bins), 0) % 2 == 1
    for h in range(2):
        for c in range(n_col):
            left = blocks[c, h]
            swapped[c, h] = jnp.where(odd, pltpu.roll(left, 1, 0), pltpu.roll(left, rows - 1, 0))
    table_copy.wait()
    start = lane
    group_rows = lax.broadcasted_iota(jnp.int32, (8, 1), 0)

    def one_row(index, carry):
        a = (start + index) % half
        away = base + a != row
        slot = jnp.where(away, n_col + a, col)

        scales = []
        for pair in range(n_col // 2):
            scale = jnp.zeros((8, 1), jnp.float32)
            for p in range(8):
                first = labels_ref[row * n_col * owned + pair * 4 + p // 2]
                second = labels_ref[((base + a) * n_col + col) * owned + p % 2]
                kept = mask_ref[first, second].astype(jnp.float32)
                scale = jnp.where(group_rows == p, kept, scale)
            scales.append(scale)

        @pl.when(away)
        def _():
            for h in range(2):
                arrived(n_col + a, h)

        for h in range(2):
            right = blocks[slot, h]
            right_real, right_imag = right[:, :bins], right[:, bins:]
            for c in range(n_col):
                left = blocks[c, h]
                for s in range(2):
                    if s:
                        left = swapped[c, h]
                    left_real, left_imag = left[:, :bins], left[:, bins:]
                    at = pl.ds(((h * n_col + c) * 2 + s) * rows, rows)
                    cross[at, :bins] = (
                        left_real * right_real + left_imag * right_imag
                    ).astype(jnp.bfloat16)
                    cross[at, bins:] = (
                        left_imag * right_real - left_real * right_imag
                    ).astype(jnp.bfloat16)

        tile = 512

        def one_tile(j, carry):
            at = pl.ds(pl.multiple_of(j * tile, tile), tile)
            at_imag = pl.ds(pl.multiple_of(lags + j * tile, tile), tile)
            real = jnp.dot(cross[...], table[:, at], preferred_element_type=jnp.float32)
            imag = jnp.dot(cross[...], table[:, at_imag], preferred_element_type=jnp.float32)
            inverse = jnp.minimum(lax.rsqrt(real * real + imag * imag), 2.0)

            def total(part):
                part = part.reshape(2, n_col, 2, rows // 8, 8, tile).sum(axis=(0, 3))
                out = []
                for pair in range(n_col // 2):
                    whole = []
                    for s in range(2):
                        upper, lower = part[2 * pair, s], part[2 * pair + 1, s]
                        upper = upper + pltpu.roll(upper, 4, 0)
                        lower = lower + pltpu.roll(lower, 4, 0)
                        both = jnp.where(group_rows < 4, upper, lower)
                        whole.append(
                            both
                            + jnp.where(
                                group_rows % 4 < 2, pltpu.roll(both, 6, 0), pltpu.roll(both, 2, 0)
                            )
                        )
                    straight = (group_rows % 4 == 0) | (group_rows % 4 == 3)
                    out.append(jnp.where(straight, whole[0], whole[1]))
                return out

            stack, phase_real, phase_imag = total(real), total(real * inverse), total(imag * inverse)
            for pair in range(n_col // 2):
                linear = stack[pair] * scales[pair] * (1.0 / windows)
                power = phase_real[pair] * phase_real[pair] + phase_imag[pair] * phase_imag[pair]
                linear_ref[a, pl.ds(8 * pair, 8), at] = linear
                phase_ref[a, pl.ds(8 * pair, 8), at] = linear * power * (1.0 / (windows * windows))
            return carry

        lax.fori_loop(0, lags // tile, one_tile, 0, unroll=True)
        return carry

    lax.fori_loop(0, half, one_row, 0)

    for copy in copies:
        copy.wait_send()


def on_device(n_row, n_col, table, spectra, station_block, pair_mask):
    windows_here, owned, width = spectra.shape
    half = n_row // 2
    rows = windows_here * owned
    lags = width
    first = n_col * owned
    shape = pltpu.VMEM((half, first * owned, lags), jnp.float32)
    sends = 1 + 2 * (n_col - 1) + (n_row - 1)
    linear, phase = pl.pallas_call(
        functools.partial(kernel, n_row, n_col, owned),
        out_shape=(shape, shape),
        in_specs=[
            pl.BlockSpec(memory_space=pltpu.HBM),
        ] * 4,
        out_specs=[pl.BlockSpec(memory_space=pltpu.VMEM)] * 2,
        scratch_shapes=[
            pltpu.VMEM((n_col + half, 2, rows, width), jnp.float32),
            pltpu.VMEM((n_col, 2, rows, width), jnp.float32),
            pltpu.VMEM(table.shape, jnp.bfloat16),
            pltpu.VMEM((4 * n_col * rows, width), jnp.bfloat16),
            pltpu.VMEM(spectra.shape, jnp.float32),
            pltpu.SMEM(station_block.shape, jnp.int32),
            pltpu.SMEM(pair_mask.shape, jnp.int32),
            pltpu.SemaphoreType.DMA((4,)),
            pltpu.SemaphoreType.DMA((sends,)),
            pltpu.SemaphoreType.DMA((n_col + half, 2)),
        ],
        compiler_params=pltpu.CompilerParams(
            collective_id=0, has_side_effects=True, vmem_limit_bytes=48 * 1024 * 1024
        ),
    )(
        *(
            pltpu.with_memory_space_constraint(part, pltpu.HBM)
            for part in (station_block, pair_mask, spectra, jnp.asarray(table))
        )
    )

    def placed(part):
        part = part.reshape(half, first, owned, lags)
        return part.transpose(1, 0, 2, 3)[:, :, None]

    return placed(linear), placed(phase)


def solution(mesh):
    def program(spectra, station_block, pair_mask):
        table = transform_table(spectra.shape[2] // 2)
        in_specs = (P("tm", ("group", "row", "col"), None), P("group"), P("group", None))
        out_specs = (
            P(("group", "row"), "tm", "col", None, None),
            P(("group", "row"), "tm", "col", None, None),
        )
        return jax.shard_map(
            functools.partial(on_device, mesh.shape["row"], mesh.shape["col"], table),
            mesh=mesh, in_specs=in_specs, out_specs=out_specs, check_vma=False,
        )(spectra, station_block, pair_mask)

    return program
```
